32 devices in a mesh: seq: 8 (over z, x), rep: 4 (over y, core).
Axes of the slice: x: 2, y: 2, z: 4, core: 2. Of those that a mesh axis runs over, the one named last changes fastest.
Arguments:
- states: bfloat16 [6144, 512], P(('rep', 'seq')), parts along dimension 0, may hold values from -6 to 6
- starts: int32 [1024], P(('rep', 'seq')), parts along dimension 0, may hold values from 0 to 1535, as said below
- straddle: int32 [32], P(('rep', 'seq')), parts along dimension 0, may hold values from 0 to 63, as said below
- key_weight: bfloat16 [512, 512], replicated
- out_weight: bfloat16 [512, 4096], P(None, 'seq'), may hold values from -0.25 to 0.25
- norm_gain: bfloat16 [4096], P('seq'), may hold values from 0.25 to 1.75
- attn_weight: bfloat16 [4096, 3, 4096], P(None, None, 'seq')
Outputs:
- attended: bfloat16 [1024, 4096], P(('rep', 'seq')), parts along dimension 0
The draws below stay inside these ranges and needn't reach their ends.
There are 4 independent parts, one for each index of `rep`. The reference program is written for one: setup_inputs(seed, part) draws one part's arguments, and reference() takes and returns one part's arrays. A program takes and returns all parts, laid end to end along the dimension named above; an argument that names none is the same for every part. Nothing has to cross between parts.
Inputs may be any that keep to these rules, and one draw needn't show every extreme that they name: Rising; shard s of 192 bytes holds the starts of exactly 32 patches, numbers s * 32 to (s+1) * 32 - 1; the first of them lies at most 63 bytes into the shard, and at byte 0 for shard 0. `straddle`: entry s equals the first start of shard s+1 minus (s+1) * 192; the last entry is 0.
All inputs are finite; a program needn't handle non-finite values.
Results may differ from the reference program's by a relative error of at most 0.0096.
Values may be sent and summed in bfloat16 or wider, within the bound.
A program may use at most 64 MiB of HBM per device.

```python
import jax
import jax.numpy as jnp
from jax import lax

D = 4096
HD = 128
LD = 512
LHD = 128
B_DEV = 192
P_DEV = 32
HALO = 64
H = 32
LH = 4
SHARDS = 8
NB = 1536
NP = 256


def patch_layout(key):
    shard_count = NP // P_DEV
    first_key, pick_key, other_key = jax.random.split(jax.random.fold_in(key, 7), 3)
    offsets = jax.random.randint(first_key, (shard_count,), 0, HALO)
    chosen = jax.random.randint(pick_key, (), 1, shard_count)
    shard_ids = jnp.arange(shard_count)
    offsets = jnp.where(shard_ids == chosen, HALO - 1, offsets)
    offsets = jnp.where(shard_ids == 0, 0, offsets)

    def others(sub_key):
        picked = jax.random.permutation(sub_key, B_DEV - HALO)[:P_DEV - 1]
        return jnp.sort(picked) + HALO
    extra = jax.vmap(others)(jax.random.split(other_key, shard_count))
    extra = extra.at[shard_count - 1, P_DEV - 2].set(B_DEV - 1)
    local = jnp.concatenate([offsets[:, None], extra], axis=1)
    starts = (local + shard_ids[:, None] * B_DEV).reshape(NP).astype(jnp.int32)
    straddle = jnp.concatenate([offsets[1:], jnp.zeros((1,), offsets.dtype)]).astype(jnp.int32)
    return (starts, straddle)


def draw_starts(key, part):
    return patch_layout(key)[0]


def draw_straddle(key, part):
    return patch_layout(key)[1]


def draw_key_weight(key, part):
    first_key = jax.random.fold_in(jax.random.fold_in(key, 11), 0)
    noise = jax.random.normal(first_key, (LD, LD), jnp.float32) * LD ** (-0.5)
    result = noise
    return result.astype(jnp.bfloat16)


def draw_attn_weight(key, part):
    first_key, second_key, third_key = jax.random.split(jax.random.fold_in(key, 13), 3)
    spread = D ** (-0.5)
    query_part = jax.random.normal(first_key, (D, D), jnp.float32) * spread
    value_part = jax.random.normal(third_key, (D, D), jnp.float32) * spread
    key_part = jax.random.normal(second_key, (D, D), jnp.float32) * spread
    return jnp.stack([query_part, key_part, value_part], axis=1).astype(jnp.bfloat16)


def steps_of(own_key, shape, cuts, least, largest):
    level, own = 1.0, jax.random.fold_in(own_key, 6)
    for dim, shards_of in cuts:
        heights = jnp.exp(jax.random.uniform(jax.random.fold_in(own, dim), (shards_of,), jnp.float32, least / len(cuts), largest / len(cuts)))
        level = level * jnp.repeat(heights, shape[dim] // shards_of).reshape([-1 if axis == dim else 1 for axis in range(len(shape))])
    return level


def scatter_about(rng, extent, scale, most, cuts=(), kind=jnp.bfloat16):
    entries = jax.random.normal(rng, extent, jnp.float32) * scale
    if len(cuts) > 0:
        entries = steps_of(rng, extent, cuts, -0.22, 0.18) * entries
    return jnp.clip(entries, min=-most, max=most).astype(kind)


def setup_inputs(seed: int = 0, part: int = 0) -> dict:
    arg_keys = jax.random.split(jax.random.key(seed), 8)
    part_splits = jax.random.split(jax.random.fold_in(arg_keys[7], part), 8)
    return {
        "states": scatter_about(part_splits[0], (NB, LD), 1.0, 6.0, ((0, 8),)),
        "starts": draw_starts(jax.random.fold_in(jax.random.fold_in(arg_keys[7], part), 71), part),
        "straddle": draw_straddle(jax.random.fold_in(jax.random.fold_in(arg_keys[7], part), 71), part),
        "key_weight": draw_key_weight(jax.random.fold_in(arg_keys[7], 71), part),
        "out_weight": scatter_about(arg_keys[4], (LD, D), LD ** -0.5, 0.25, ((1, 8),)),
        "norm_gain": jnp.clip(1.0 + 0.15 * jax.random.normal(arg_keys[5], (D,), jnp.float32), 0.25, 1.75).astype(jnp.bfloat16),
        "attn_weight": draw_attn_weight(jax.random.fold_in(arg_keys[7], 71), part),
    }


epsilon = 1e-05

def cross_pool(window, local_starts, halo_count, key_weight):
    window_rows = window.shape[0]
    position = jnp.arange(window_rows, dtype=jnp.int32)
    patch_ends = jnp.concatenate([local_starts[1:], (B_DEV + halo_count).reshape(1).astype(jnp.int32)])
    member = (position[None, :] >= local_starts[:, None]) & (position[None, :] < patch_ends[:, None])
    byte_count = lax.optimization_barrier(jnp.sum(member.astype(jnp.float32), axis=1))
    query = (jnp.dot(member.astype(jnp.bfloat16), window, preferred_element_type=jnp.float32) / byte_count[:, None]).astype(jnp.bfloat16)
    keys = jnp.dot(window, key_weight, preferred_element_type=jnp.float32).astype(jnp.bfloat16)
    query_heads = query.astype(jnp.float32).reshape(P_DEV, LH, LHD)
    key_heads = keys.astype(jnp.float32).reshape(window_rows, LH, LHD)
    scores = jnp.einsum('phd,jhd->hpj', query_heads, key_heads) / jnp.sqrt(jnp.float32(LHD))
    scores = jnp.where(member[None], scores, jnp.float32(-1e+30))
    row_peak = lax.optimization_barrier(jnp.max(scores, axis=-1, keepdims=True))
    expo = jnp.where(member[None], jnp.exp(scores - row_peak), jnp.float32(0.0))
    cross = (expo / lax.optimization_barrier(jnp.sum(expo, axis=-1, keepdims=True))).astype(jnp.bfloat16)
    value_heads = window.astype(jnp.float32).reshape(window_rows, LH, LHD)
    pooled = jnp.einsum('hpj,jhd->phd', cross.astype(jnp.float32), value_heads)
    return pooled.reshape(P_DEV, LD).astype(jnp.bfloat16)

def reference(states, starts, straddle, key_weight, out_weight, norm_gain, attn_weight):
    padded = jnp.concatenate([states, jnp.zeros((HALO, LD), states.dtype)], axis=0)
    start_table = starts.reshape(SHARDS, P_DEV)

    def one_shard(shard):
        window = lax.dynamic_slice_in_dim(padded, (shard * B_DEV).astype(jnp.int32), B_DEV + HALO, 0)
        local_starts = (start_table[shard] - shard * B_DEV).astype(jnp.int32)
        return cross_pool(window, local_starts, straddle[shard], key_weight)
    pooled = lax.map(one_shard, jnp.arange(SHARDS, dtype=jnp.int32)).reshape(NP, LD)
    embedding = jnp.dot(pooled, out_weight, preferred_element_type=jnp.float32)
    meansq = lax.optimization_barrier(jnp.mean(embedding * embedding, axis=1, keepdims=True))
    normed = (embedding * lax.rsqrt(meansq + epsilon) * norm_gain.astype(jnp.float32)[None, :]).astype(jnp.bfloat16)
    projected = jnp.dot(normed, attn_weight.reshape(D, 3 * D), preferred_element_type=jnp.float32).astype(jnp.bfloat16)
    head_view = projected.astype(jnp.float32).reshape(NP, 3, H, HD)
    scores = jnp.einsum('qhd,khd->hqk', head_view[:, 0], head_view[:, 1]) / jnp.sqrt(jnp.float32(HD))
    causal = jnp.arange(NP)[:, None] >= jnp.arange(NP)[None, :]
    scores = jnp.where(causal[None], scores, jnp.float32(-1e+30))
    row_peak = lax.optimization_barrier(jnp.max(scores, axis=-1, keepdims=True))
    expo = jnp.where(causal[None], jnp.exp(scores - row_peak), jnp.float32(0.0))
    probs = (expo / lax.optimization_barrier(jnp.sum(expo, axis=-1, keepdims=True))).astype(jnp.bfloat16)
    attended = jnp.einsum('hqk,khd->qhd', probs.astype(jnp.float32), head_view[:, 2])
    return attended.reshape(NP, D).astype(jnp.bfloat16)
```

```python
import functools
import math

import jax
import jax.numpy as jnp
from jax import lax
from jax.experimental import pallas as pl
from jax.experimental.pallas import tpu as pltpu
from jax.sharding import PartitionSpec as P

HD = 128
LHD = 128
HALO = 64
CORES = 2
PAD = 16

epsilon = 1e-05

BF16 = jnp.bfloat16
F32 = jnp.float32


def dot(a, b):
    return jnp.dot(a, b, preferred_element_type=F32)


def dot_t(a, b):
    return lax.dot_general(a, b, (((1,), (1,)), ((), ())), preferred_element_type=F32)


def softmax_dot(scores, keep, values):
    scores = jnp.where(keep, scores, F32(-1e30))
    peak = jnp.max(scores, axis=-1, keepdims=True)
    expo = jnp.where(keep, jnp.exp(scores - peak), F32(0.0))
    total = jnp.sum(expo, axis=-1, keepdims=True)
    return dot((expo / total).astype(BF16), values).astype(BF16)


def kernel(
    nz, nx, ny,
    states, starts, straddle, key_weight, out_weight, gain, attn_weight,
    out,
    window, kw, ow, w, pg, acc, att,
    l_sem, w_sem, h_sem,
    zs_sem, xs_sem, m_sem, ys_sem, yr_sem, cs_sem, cr_sem,
    ps_sem, pr_sem, as_sem, ar_sem,
):
    n = nz * nx
    s = lax.axis_index("seq")
    r = lax.axis_index("rep")
    zi, xi = s // nx, s % nx
    yi, ci = r // CORES, r % CORES
    other = yi * CORES + (1 - ci)
    rows, width = states.shape
    patches = starts.shape[1]
    cols = out_weight.shape[2]
    heads = cols // HD
    model = cols * n

    def seq_of(kz, kx):
        return ((zi + nz + kz) % nz) * nx + (xi + nx + kx) % nx

    def rep_of(ky):
        return ((yi + ny + ky) % ny) * CORES + ci

    def remote(src, dst, send, recv, seq, rep):
        return pltpu.make_async_remote_copy(
            src_ref=src, dst_ref=dst, send_sem=send, recv_sem=recv,
            device_id={"seq": seq, "rep": rep}, device_id_type=pl.DeviceIdType.MESH,
        )

    barrier = pltpu.get_barrier_semaphore()

    def greet(seq, rep):
        pl.semaphore_signal(
            barrier, inc=1, device_id={"seq": seq, "rep": rep},
            device_id_type=pl.DeviceIdType.MESH,
        )

    for k in range(1, n):
        greet((s + k) % n, r)
    for k in range(1, ny):
        greet(s, rep_of(k))
    greet(s, other)

    local = [
        pltpu.make_async_copy(states, window.at[pl.ds(0, rows)], l_sem.at[0]),
        pltpu.make_async_copy(key_weight, kw, l_sem.at[1]),
        pltpu.make_async_copy(out_weight, ow.at[s], l_sem.at[2]),
    ]
    for copy in local:
        copy.start()
    w_copy = pltpu.make_async_copy(attn_weight, w, w_sem)
    w_copy.start()

    pl.semaphore_wait(barrier, n - 1 + ny - 1 + 1)

    left = (s + n - 1) % n
    halo = remote(
        states.at[pl.ds(0, HALO)], window.at[pl.ds(rows, HALO)],
        h_sem.at[0], h_sem.at[1], left, r,
    )

    @pl.when(s > 0)
    def _():
        halo.start()

    sent = []

    def go(copy):
        copy.start()
        sent.append(copy)

    mine = out_weight.at[r]
    for kx in range(1, nx):
        go(remote(mine, ow.at[s, r], xs_sem.at[0, kx], m_sem.at[0, kx], seq_of(0, kx), r))
    for kz in range(1, nz):
        go(remote(mine, ow.at[s, r], zs_sem.at[kz], m_sem.at[kz, 0], seq_of(kz, 0), r))

    @pl.when(s == n - 1)
    def _():
        window[pl.ds(rows, HALO), :] = jnp.zeros((HALO, width), BF16)

    square0 = lax.broadcasted_iota(jnp.int32, (patches, patches), 0)
    square1 = lax.broadcasted_iota(jnp.int32, (patches, patches), 1)
    first = (starts[...] - s * rows).astype(F32)
    low = jnp.sum(jnp.where(square0 == square1, first, 0.0), axis=1, keepdims=True)
    high = jnp.sum(jnp.where(square0 + 1 == square1, first, 0.0), axis=1, keepdims=True)
    line = lax.broadcasted_iota(jnp.int32, (patches, 1), 0)
    high = jnp.where(line == patches - 1, (rows + straddle[0]).astype(F32), high)
    place = lax.broadcasted_iota(jnp.int32, (patches, rows + HALO), 1).astype(F32)
    member = (place >= low) & (place < high)
    count = high - low

    local[0].wait()
    local[1].wait()

    @pl.when(s < n - 1)
    def _():
        halo.wait_recv()

    whole = window[...]
    keys = dot(whole, kw[...]).astype(BF16)
    query = (dot(member.astype(BF16), whole) / count).astype(BF16)
    scale = F32(1.0 / math.sqrt(LHD))
    for h in range(width // LHD):
        part = slice(h * LHD, (h + 1) * LHD)
        pg[s, pl.ds(0, patches), part] = softmax_dot(
            dot_t(query[:, part], keys[:, part]) * scale, member, whole[:, part]
        )
    pg[s, pl.ds(patches, PAD), pl.ds(0, cols)] = jnp.broadcast_to(gain[...], (PAD, cols))
    for k in range(1, n):
        go(remote(pg.at[s], pg.at[s], ps_sem.at[k], pr_sem.at[k], (s + k) % n, r))

    def wait_for(ref, sem):
        pltpu.make_async_copy(ref, ref, sem).wait()

    order = [(kz, kx) for kx in range(nx) for kz in range(nz)][1:]
    if nx > 1:
        order = [(0, kx) for kx in range(1, nx)] + [o for o in order if o[0] > 0]
    for kz, kx in order:
        j = seq_of(-kz, -kx)
        piece = ow.at[j, r]
        wait_for(piece, m_sem.at[kz, kx])
        for ky in range(1, ny):
            go(remote(piece, piece, ys_sem.at[ky, kz, kx], yr_sem.at[ky, kz, kx], s, rep_of(ky)))
        if kx == 0:
            for k in range(1, nx):
                go(remote(piece, piece, xs_sem.at[kz, k], m_sem.at[kz, k], seq_of(0, k), r))
        go(remote(piece, piece, cs_sem.at[0, kz, kx], cr_sem.at[0, kz, kx], s, other))

    for k in range(1, n):
        wait_for(pg.at[s], pr_sem.at[k])
    pooled = pg[:, pl.ds(0, patches), :].reshape(n * patches, width)

    def project(j, squares, fresh):
        weight = ow[j].reshape(width, cols)
        embed = dot(pooled, weight)
        squares = squares + jnp.sum(embed * embed, axis=1, keepdims=True)
        row = pg[j, pl.ds(patches, PAD), pl.ds(0, cols)][0:1, :].astype(F32)
        scaled = (embed * row).astype(BF16)
        for t in range(3):
            span = slice(t * cols, (t + 1) * cols)
            term = dot(scaled, w[t, j])
            if fresh:
                acc[:, span] = term
            else:
                acc[:, span] = acc[:, span] + term
        return squares

    def arrived(kz, kx):
        j = seq_of(-kz, -kx)
        for ky in range(ny):
            wait_for(ow.at[j, other], cr_sem.at[ky, kz, kx])
        return j

    local[2].wait()
    w_copy.wait()
    squares = project(s, jnp.zeros((n * patches, 1), F32), True)
    before = None
    for kz, kx in order:
        j = seq_of(-kz, -kx)
        for ky in range(1, ny):
            piece = ow.at[j, rep_of(-ky)]
            wait_for(piece, yr_sem.at[ky, kz, kx])
            go(remote(piece, piece, cs_sem.at[ky, kz, kx], cr_sem.at[ky, kz, kx], s, other))
        if before is not None:
            squares = project(arrived(*before), squares, False)
        before = (kz, kx)
    if before is not None:
        squares = project(arrived(*before), squares, False)

    total = n * patches
    rstd = lax.rsqrt(squares / F32(model) + epsilon)
    causal = lax.broadcasted_iota(jnp.int32, (total, total), 0) >= lax.broadcasted_iota(
        jnp.int32, (total, total), 1
    )
    scale = F32(1.0 / math.sqrt(HD))
    own = []
    for h in range(heads):
        q, k, v = (
            (acc[:, t * cols + h * HD : t * cols + (h + 1) * HD] * rstd).astype(BF16)
            for t in range(3)
        )
        att[h] = softmax_dot(dot_t(q, k) * scale, causal, v).reshape(n, patches, HD)
        span = pl.ds(pl.multiple_of(s * cols + h * HD, HD), HD)
        for k in range(1, n):
            j = (s + k) % n
            go(remote(att.at[h, j], out.at[:, span], as_sem.at[h, k], ar_sem.at[h, k], j, r))
        own.append(pltpu.make_async_copy(att.at[h, s], out.at[:, span], as_sem.at[h, 0]))
        own[-1].start()

    for copy in own:
        copy.wait()
    for h in range(heads):
        for k in range(1, n):
            span = pl.ds(pl.multiple_of(((s + n - k) % n) * cols + h * HD, HD), HD)
            wait_for(out.at[:, span], ar_sem.at[h, k])
    for copy in sent:
        copy.wait_send()

    @pl.when(s > 0)
    def _():
        halo.wait_send()


def split_seq(n):
    power = 1
    while power * power < n:
        power *= 2
    return (power, n // power) if n % power == 0 else (n, 1)


def shards(states, starts, straddle, key_weight, out_weight, norm_gain, attn_weight):
    n, reps = lax.axis_size("seq"), lax.axis_size("rep")
    nz, nx = split_seq(n)
    ny = reps // CORES
    rows, width = states.shape
    patches = starts.shape[0]
    model, three, cols = attn_weight.shape
    heads = cols // HD
    total = n * patches
    w = attn_weight.transpose(1, 0, 2).reshape(three, n, model // n, cols)
    any_space = pl.BlockSpec(memory_space=pl.ANY)
    vmem = pl.BlockSpec(memory_space=pltpu.VMEM)
    smem = pl.BlockSpec(memory_space=pltpu.SMEM)
    dma = pltpu.SemaphoreType.DMA
    flops = 2 * total * (model * three * cols + width * model)
    return pl.pallas_call(
        functools.partial(kernel, nz, nx, ny),
        out_shape=jax.ShapeDtypeStruct((patches, model), BF16),
        in_specs=[any_space, vmem, smem, any_space, any_space, vmem, any_space],
        out_specs=any_space,
        scratch_shapes=[
            pltpu.VMEM((rows + HALO, width), BF16),
            pltpu.VMEM(key_weight.shape, BF16),
            pltpu.VMEM((n, reps, width // reps, cols), BF16),
            pltpu.VMEM(w.shape, BF16),
            pltpu.VMEM((n, patches + PAD, width), BF16),
            pltpu.VMEM((total, three * cols), F32),
            pltpu.VMEM((heads, n, patches, HD), BF16),
            dma((3,)), dma, dma((2,)),
            dma((nz,)), dma((nz, nx)), dma((nz, nx)),
            dma((ny, nz, nx)), dma((ny, nz, nx)), dma((ny, nz, nx)), dma((ny, nz, nx)),
            dma((n,)), dma((n,)), dma((heads, n)), dma((heads, n)),
        ],
        compiler_params=pltpu.CompilerParams(
            collective_id=0, has_side_effects=True, vmem_limit_bytes=48 * 1024 * 1024
        ),
        cost_estimate=pl.CostEstimate(
            flops=flops, bytes_accessed=w.size * 2, transcendentals=0
        ),
    )(
        states, starts.reshape(1, patches), straddle, key_weight,
        out_weight.reshape(reps, width // reps, cols), norm_gain.reshape(1, cols), w,
    )


def solution(mesh):
    placed = (
        P(("rep", "seq"), None),
        P(("rep", "seq")),
        P(("rep", "seq")),
        P(),
        P(None, "seq"),
        P("seq"),
        P(None, None, "seq"),
    )
    return jax.shard_map(
        shards, mesh=mesh, in_specs=placed, out_specs=P(("rep", "seq"), None), check_vma=False
    )
```

```python
import functools
import math

import jax
import jax.numpy as jnp
from jax import lax
from jax.experimental import pallas as pl
from jax.experimental.pallas import tpu as pltpu
from jax.sharding import PartitionSpec as P

HD = 128
LHD = 128
HALO = 64
CORES = 2

epsilon = 1e-05

BF16 = jnp.bfloat16
F32 = jnp.float32


def dot(a, b):
    return jnp.dot(a, b, preferred_element_type=F32)


def dot_t(a, b):
    return lax.dot_general(a, b, (((1,), (1,)), ((), ())), preferred_element_type=F32)


def softmax_dot(scores, keep, values):
    scores = jnp.where(keep, scores, F32(-1e30))
    peak = jnp.max(scores, axis=-1, keepdims=True)
    expo = jnp.where(keep, jnp.exp(scores - peak), F32(0.0))
    total = jnp.sum(expo, axis=-1, keepdims=True)
    return dot((expo / total).astype(BF16), values).astype(BF16)


def kernel(
    nz, nx, ny,
    states, starts, straddle, key_weight, out_weight, gain, attn_weight,
    out,
    window, kw, ow, w, pg, gv, gs, st, acc, att,
    l_sem, w_sem, h_sem,
    zs_sem, xs_sem, m_sem, ys_sem, yr_sem, cs_sem, cr_sem,
    ps_sem, pr_sem, gs_sem, gr_sem, as_sem, ar_sem,
):
    n = nz * nx
    s = lax.axis_index("seq")
    r = lax.axis_index("rep")
    zi, xi = s // nx, s % nx
    yi, ci = r // CORES, r % CORES
    other = yi * CORES + (1 - ci)
    rows, width = states.shape
    patches = starts.shape[0]
    cols = out_weight.shape[3]
    heads = cols // HD
    model = cols * n

    def flip(index, mask):
        bit = 1
        for _ in range(mask.bit_length()):
            if mask & bit:
                index = index + (1 - 2 * ((index // bit) % 2)) * bit
            bit *= 2
        return index

    def seq_of(kz, kx):
        return flip(zi, kz) * nx + (xi + nx + kx) % nx

    def y_of(ky):
        return (yi + ny + ky) % ny

    def rep_of(ky):
        return y_of(ky) * CORES + ci

    def remote(src, dst, send, recv, seq, rep):
        return pltpu.make_async_remote_copy(
            src_ref=src, dst_ref=dst, send_sem=send, recv_sem=recv,
            device_id={"seq": seq, "rep": rep}, device_id_type=pl.DeviceIdType.MESH,
        )

    barrier = pltpu.get_barrier_semaphore()

    def greet(seq, rep):
        pl.semaphore_signal(
            barrier, inc=1, device_id={"seq": seq, "rep": rep},
            device_id_type=pl.DeviceIdType.MESH,
        )

    for k in range(1, n):
        greet((s + k) % n, r)
    for k in range(1, ny):
        greet(s, rep_of(k))
    greet(s, other)

    local = [
        pltpu.make_async_copy(states, window.at[pl.ds(0, rows)], l_sem.at[0]),
        pltpu.make_async_copy(starts, st, l_sem.at[1]),
        pltpu.make_async_copy(gain, gv, l_sem.at[2]),
        pltpu.make_async_copy(key_weight, kw, l_sem.at[3]),
        pltpu.make_async_copy(out_weight, ow.at[s], l_sem.at[4]),
    ]
    for copy in local:
        copy.start()
    w_copy = pltpu.make_async_copy(attn_weight, w, w_sem)
    w_copy.start()
    local[2].wait()
    gs[s] = gv[...].astype(F32).reshape(1, cols)

    pl.semaphore_wait(barrier, n - 1 + ny - 1 + 1)

    left = (s + n - 1) % n
    halo = remote(
        states.at[pl.ds(0, HALO)], window.at[pl.ds(rows, HALO)],
        h_sem.at[0], h_sem.at[1], left, r,
    )

    @pl.when(s > 0)
    def _():
        halo.start()

    sent = []

    def go(copy):
        copy.start()
        sent.append(copy)

    full = [(0, kx) for kx in range(1, nx)] + ([(1, 0)] if nz > 1 else [])
    z_order = list(range(2, nz)) + ([1] if nz > 1 else [])

    def block(ref, j, o):
        return ref.at[j, ci] if o in full else ref.at[j, ci, yi]

    for kz in z_order:
        o = (kz, 0)
        source = out_weight.at[ci] if o in full else out_weight.at[ci, yi]
        go(remote(source, block(ow, s, o), zs_sem.at[kz], m_sem.at[kz, 0], seq_of(kz, 0), r))
    for kx in range(1, nx):
        go(remote(out_weight.at[ci], ow.at[s, ci], xs_sem.at[0, kx], m_sem.at[0, kx], seq_of(0, kx), r))
    for k in range(1, n):
        go(remote(gs.at[s], gs.at[s], gs_sem.at[k], gr_sem.at[k], (s + k) % n, r))

    @pl.when(s == n - 1)
    def _():
        window[pl.ds(rows, HALO), :] = jnp.zeros((HALO, width), BF16)

    square0 = lax.broadcasted_iota(jnp.int32, (patches, patches), 0)
    square1 = lax.broadcasted_iota(jnp.int32, (patches, patches), 1)
    local[1].wait()
    first = (st[...].reshape(1, patches) - s * rows).astype(F32)
    low = jnp.sum(jnp.where(square0 == square1, first, 0.0), axis=1, keepdims=True)
    high = jnp.sum(jnp.where(square0 + 1 == square1, first, 0.0), axis=1, keepdims=True)
    line = lax.broadcasted_iota(jnp.int32, (patches, 1), 0)
    high = jnp.where(line == patches - 1, (rows + straddle[0]).astype(F32), high)
    place = lax.broadcasted_iota(jnp.int32, (patches, rows + HALO), 1).astype(F32)
    member = (place >= low) & (place < high)
    count = high - low

    local[0].wait()
    local[3].wait()

    @pl.when(s < n - 1)
    def _():
        halo.wait_recv()

    whole = window[...]
    keys = dot(whole, kw[...]).astype(BF16)
    query = (dot(member.astype(BF16), whole) / count).astype(BF16)
    scale = F32(1.0 / math.sqrt(LHD))
    for h in range(width // LHD):
        part = slice(h * LHD, (h + 1) * LHD)
        pg[s, :, part] = softmax_dot(
            dot_t(query[:, part], keys[:, part]) * scale, member, whole[:, part]
        )
    for kz in z_order:
        go(remote(pg.at[s], pg.at[s], ps_sem.at[kz, 0], pr_sem.at[kz, 0], seq_of(kz, 0), r))
    for kx in range(1, nx):
        go(remote(pg.at[s], pg.at[s], ps_sem.at[0, kx], pr_sem.at[0, kx], seq_of(0, kx), r))

    def wait_for(ref, sem):
        pltpu.make_async_copy(ref, ref, sem).wait()

    def pass_on(o):
        kz, kx = o
        j = seq_of(kz, -kx)
        got = block(ow, j, o)
        piece = ow.at[j, ci, yi]
        wait_for(got, m_sem.at[kz, kx])
        if o not in full:
            for ky in range(1, ny):
                go(remote(piece, piece, ys_sem.at[ky, kz, kx], yr_sem.at[ky, kz, kx], s, rep_of(ky)))
        if kx == 0:
            for k in range(1, nx):
                go(remote(piece, piece, xs_sem.at[kz, k], m_sem.at[kz, k], seq_of(0, k), r))
        go(remote(got, got, cs_sem.at[0, kz, kx], cr_sem.at[0, kz, kx], s, other))

    def pass_y(o):
        kz, kx = o
        for ky in range(1, ny):
            piece = ow.at[seq_of(kz, -kx), ci, y_of(-ky)]
            wait_for(piece, yr_sem.at[ky, kz, kx])
            go(remote(piece, piece, cs_sem.at[ky, kz, kx], cr_sem.at[ky, kz, kx], s, other))

    def arrived(o):
        kz, kx = o
        j = seq_of(kz, -kx)
        if o in full:
            wait_for(ow.at[j, 1 - ci], cr_sem.at[0, kz, kx])
        else:
            for ky in range(ny):
                wait_for(ow.at[j, 1 - ci, y_of(-ky)], cr_sem.at[ky, kz, kx])
        return j

    for kz in z_order:
        if (kz, 0) in full:
            continue
        pass_on((kz, 0))
    for kz in z_order:
        j = seq_of(kz, 0)
        wait_for(pg.at[j], pr_sem.at[kz, 0])
        for kx in range(1, nx):
            go(remote(pg.at[j], pg.at[j], ps_sem.at[kz, kx], pr_sem.at[kz, kx], seq_of(0, kx), r))
    for o in full[::-1]:
        pass_on(o)

    for kz in range(nz):
        for kx in range(1, nx):
            wait_for(pg.at[s], pr_sem.at[kz, kx])
    for k in range(1, n):
        wait_for(gs.at[s], gr_sem.at[k])
    pooled = pg[...].reshape(n * patches, width)

    def project(j, squares, fresh):
        weight = ow[j].reshape(width, cols)
        embed = dot(pooled, weight)
        squares = squares + jnp.sum(embed * embed, axis=1, keepdims=True)
        scaled = (embed * gs[j]).astype(BF16)
        for t in range(3):
            span = slice(t * cols, (t + 1) * cols)
            term = dot(scaled, w[t, j])
            if fresh:
                acc[:, span] = term
            else:
                acc[:, span] = acc[:, span] + term
        return squares

    late = [(kz, kx) for kz in z_order for kx in range(1, nx)]
    early = [(kz, 0) for kz in z_order if (kz, 0) not in full]
    ready, waiting = list(full), early + late
    steps = []
    for i, o in enumerate(late):
        steps.append((pass_on, o))
        if i < len(early):
            steps.append((pass_y, o := early[i]))
        if ready:
            steps.append((None, ready.pop(0)))
        if i < len(early):
            ready.append(o)
            waiting.remove(o)
    for o in waiting:
        steps.append((pass_y, o))
        if ready:
            steps.append((None, ready.pop(0)))
        ready.append(o)
    steps += [(None, o) for o in ready]

    local[4].wait()
    w_copy.wait()
    squares = project(s, jnp.zeros((n * patches, 1), F32), True)
    for act, o in steps:
        if act is None:
            squares = project(arrived(o), squares, False)
        else:
            act(o)

    total = n * patches
    rstd = lax.rsqrt(squares / F32(model) + epsilon)
    causal = lax.broadcasted_iota(jnp.int32, (total, total), 0) >= lax.broadcasted_iota(
        jnp.int32, (total, total), 1
    )
    scale = F32(1.0 / math.sqrt(HD))
    own = []
    for h in range(heads):
        q, k, v = (
            (acc[:, t * cols + h * HD : t * cols + (h + 1) * HD] * rstd).astype(BF16)
            for t in range(3)
        )
        att[h] = softmax_dot(dot_t(q, k) * scale, causal, v).reshape(n, patches, HD)
        span = pl.ds(pl.multiple_of(s * cols + h * HD, HD), HD)
        for k in range(1, n):
            j = (s + k) % n
            go(remote(att.at[h, j], out.at[:, span], as_sem.at[h, k], ar_sem.at[h, k], j, r))
        own.append(pltpu.make_async_copy(att.at[h, s], out.at[:, span], as_sem.at[h, 0]))
        own[-1].start()

    for copy in own:
        copy.wait()
    for h in range(heads):
        for k in range(1, n):
            span = pl.ds(pl.multiple_of(((s + n - k) % n) * cols + h * HD, HD), HD)
            wait_for(out.at[:, span], ar_sem.at[h, k])
    for copy in sent:
        copy.wait_send()

    @pl.when(s > 0)
    def _():
        halo.wait_send()


def split_seq(n):
    power = 1
    while power * power < n:
        power *= 2
    return (power, n // power) if n % power == 0 else (n, 1)


def shards(states, starts, straddle, key_weight, out_weight, norm_gain, attn_weight):
    n, reps = lax.axis_size("seq"), lax.axis_size("rep")
    nz, nx = split_seq(n)
    ny = reps // CORES
    rows, width = states.shape
    patches = starts.shape[0]
    model, three, cols = attn_weight.shape
    heads = cols // HD
    total = n * patches
    w = attn_weight.transpose(1, 0, 2).reshape(three, n, model // n, cols)
    any_space = pl.BlockSpec(memory_space=pl.ANY)
    smem = pl.BlockSpec(memory_space=pltpu.SMEM)
    dma = pltpu.SemaphoreType.DMA
    flops = 2 * total * (model * three * cols + width * model)
    return pl.pallas_call(
        functools.partial(kernel, nz, nx, ny),
        out_shape=jax.ShapeDtypeStruct((patches, model), BF16),
        in_specs=[any_space, any_space, smem, any_space, any_space, any_space, any_space],
        out_specs=any_space,
        scratch_shapes=[
            pltpu.VMEM((rows + HALO, width), BF16),
            pltpu.VMEM(key_weight.shape, BF16),
            pltpu.VMEM((n, CORES, ny, width // reps, cols), BF16),
            pltpu.VMEM(w.shape, BF16),
            pltpu.VMEM((n, patches, width), BF16),
            pltpu.VMEM((cols,), BF16),
            pltpu.VMEM((n, 1, cols), F32),
            pltpu.VMEM((patches,), jnp.int32),
            pltpu.VMEM((total, three * cols), F32),
            pltpu.VMEM((heads, n, patches, HD), BF16),
            dma((5,)), dma, dma((2,)),
            dma((nz,)), dma((nz, nx)), dma((nz, nx)),
            dma((ny, nz, nx)), dma((ny, nz, nx)), dma((ny, nz, nx)), dma((ny, nz, nx)),
            dma((nz, nx)), dma((nz, nx)), dma((n,)), dma((n,)), dma((heads, n)), dma((heads, n)),
        ],
        compiler_params=pltpu.CompilerParams(
            collective_id=0, has_side_effects=True, vmem_limit_bytes=60 * 1024 * 1024
        ),
        cost_estimate=pl.CostEstimate(
            flops=flops, bytes_accessed=w.size * 2, transcendentals=0
        ),
    )(
        states, starts, straddle, key_weight,
        out_weight.reshape(CORES, ny, width // reps, cols), norm_gain, w,
    )


def solution(mesh):
    placed = (
        P(("rep", "seq"), None),
        P(("rep", "seq")),
        P(("rep", "seq")),
        P(),
        P(None, "seq"),
        P("seq"),
        P(None, None, "seq"),
    )
    return jax.shard_map(
        shards, mesh=mesh, in_specs=placed, out_specs=P(("rep", "seq"), None), check_vma=False
    )
```

```python
import functools
import math

import jax
import jax.numpy as jnp
from jax import lax
from jax.experimental import pallas as pl
from jax.experimental.pallas import tpu as pltpu
from jax.sharding import PartitionSpec as P

HD = 128
LHD = 128
HALO = 64
CORES = 2

epsilon = 1e-05

BF16 = jnp.bfloat16
F32 = jnp.float32


def dot(a, b):
    return jnp.dot(a, b, preferred_element_type=F32)


def dot_t(a, b):
    return lax.dot_general(a, b, (((1,), (1,)), ((), ())), preferred_element_type=F32)


def softmax_dot(scores, keep, values):
    scores = jnp.where(keep, scores, F32(-1e30))
    peak = jnp.max(scores, axis=-1, keepdims=True)
    expo = jnp.where(keep, jnp.exp(scores - peak), F32(0.0))
    total = jnp.sum(expo, axis=-1, keepdims=True)
    return dot((expo / total).astype(BF16), values).astype(BF16)


def kernel(
    nz, nx, ny,
    states, starts, straddle, key_weight, out_weight, gain, attn_weight,
    out,
    window, kw, ow, w, pg, gv, gs, st, acc, att,
    l_sem, w_sem, h_sem,
    zs_sem, zr_sem, xs_sem, xr_sem, es_sem, er_sem, ys_sem, yr_sem, cs_sem, cr_sem,
    ps_sem, pr_sem, gs_sem, gr_sem, as_sem, ar_sem,
):
    n = nz * nx
    s = lax.axis_index("seq")
    r = lax.axis_index("rep")
    zi, xi = s // nx, s % nx
    yi, ci = r // CORES, r % CORES
    other = yi * CORES + (1 - ci)
    rows, width = states.shape
    patches = starts.shape[0]
    cols = out_weight.shape[3]
    heads = cols // HD
    model = cols * n

    def flip(index, mask):
        bit = 1
        for _ in range(mask.bit_length()):
            if mask & bit:
                index = index + (1 - 2 * ((index // bit) % 2)) * bit
            bit *= 2
        return index

    def seq_of(kz, kx):
        return flip(zi, kz) * nx + (xi + nx + kx) % nx

    def y_of(ky):
        return (yi + ny + ky) % ny

    def rep_of(ky):
        return y_of(ky) * CORES + ci

    def remote(src, dst, send, recv, seq, rep):
        return pltpu.make_async_remote_copy(
            src_ref=src, dst_ref=dst, send_sem=send, recv_sem=recv,
            device_id={"seq": seq, "rep": rep}, device_id_type=pl.DeviceIdType.MESH,
        )

    barrier = pltpu.get_barrier_semaphore()

    def greet(seq, rep):
        pl.semaphore_signal(
            barrier, inc=1, device_id={"seq": seq, "rep": rep},
            device_id_type=pl.DeviceIdType.MESH,
        )

    for k in range(1, n):
        greet((s + k) % n, r)
    for k in range(1, ny):
        greet(s, rep_of(k))
    greet(s, other)

    local = [
        pltpu.make_async_copy(states, window.at[pl.ds(0, rows)], l_sem.at[0]),
        pltpu.make_async_copy(starts, st, l_sem.at[1]),
        pltpu.make_async_copy(gain, gv, l_sem.at[2]),
        pltpu.make_async_copy(key_weight, kw, l_sem.at[3]),
        pltpu.make_async_copy(out_weight, ow.at[s], l_sem.at[4]),
    ]
    for copy in local:
        copy.start()
    w_copy = pltpu.make_async_copy(attn_weight, w, w_sem)
    w_copy.start()
    local[2].wait()
    gs[s] = gv[...].astype(F32).reshape(1, cols)

    pl.semaphore_wait(barrier, n - 1 + ny - 1 + 1)

    left = (s + n - 1) % n
    halo = remote(
        states.at[pl.ds(0, HALO)], window.at[pl.ds(rows, HALO)],
        h_sem.at[0], h_sem.at[1], left, r,
    )

    @pl.when(s > 0)
    def _():
        halo.start()

    sent, maybe = [], []

    def go(copy):
        copy.start()
        sent.append(copy)

    def go_if(cond, copy):
        @pl.when(cond)
        def _():
            copy.start()

        maybe.append((cond, copy))

    even = 1 - zi % 2
    short = jnp.minimum(zi, nz - 1 - zi)

    def near(t):
        if t == 0:
            return zi
        ahead = even if t % 2 == 1 else 1 - even
        both = zi + (2 * ahead - 1) * ((t + 1) // 2)
        lone = jnp.where(zi * 2 < nz, zi + t - short, zi - t + short)
        return jnp.where(t <= 2 * short, both, lone)

    line_z = [near(t) for t in range(nz)]

    def shard_of(o):
        return line_z[o[0]] * nx + (xi + nx - o[1]) % nx

    def wait_for(ref, sem):
        pltpu.make_async_copy(ref, ref, sem).wait()

    whole_ones = [(0, kx) for kx in range(1, nx)] + ([(1, 0)] if nz > 1 else [])

    mine = out_weight.at[ci, yi]
    for side in range(2):
        z_to = zi + 2 * side - 1
        go_if(
            (z_to >= 0) & (z_to < nz),
            remote(mine, ow.at[s, ci, yi], zs_sem.at[0, side], zr_sem.at[zi], z_to * nx + xi, r),
        )
    for k in range(1, nx):
        go(remote(mine, ow.at[s, ci, yi], xs_sem.at[0, k], xr_sem.at[0, k], seq_of(0, k), r))

    def send_rest(k, seq):
        for ky in range(1, ny):
            part = y_of(-ky)
            go(remote(out_weight.at[ci, part], ow.at[s, ci, part], es_sem.at[k, ky], er_sem.at[k, ky], seq, r))

    def pass_first(o):
        t, kx = o
        j = shard_of(o)
        piece = ow.at[j, ci, yi]
        wait_for(piece, zr_sem.at[line_z[t]] if kx == 0 else xr_sem.at[t, kx])
        if kx == 0:
            z_to = jnp.where(line_z[t] < zi, zi + 1, zi - 1)
            go_if(
                (z_to >= 0) & (z_to < nz),
                remote(piece, piece, zs_sem.at[t, 0], zr_sem.at[line_z[t]], z_to * nx + xi, r),
            )
            for k in range(1, nx):
                go(remote(piece, piece, xs_sem.at[t, k], xr_sem.at[t, k], seq_of(0, k), r))
        if o not in whole_ones:
            for ky in range(1, ny):
                go(remote(piece, piece, ys_sem.at[ky, t, kx], yr_sem.at[ky, t, kx], s, rep_of(ky)))
        go(remote(piece, piece, cs_sem.at[0, t, kx], cr_sem.at[0, t, kx], s, other))

    def pass_rest(o):
        t, kx = o
        for ky in range(1, ny):
            piece = ow.at[shard_of(o), ci, y_of(-ky)]
            wait_for(piece, er_sem.at[kx, ky] if o in whole_ones else yr_sem.at[ky, t, kx])
            go(remote(piece, piece, cs_sem.at[ky, t, kx], cr_sem.at[ky, t, kx], s, other))

    def arrived(o):
        t, kx = o
        j = shard_of(o)
        for ky in range(ny):
            wait_for(ow.at[j, 1 - ci, y_of(-ky)], cr_sem.at[ky, t, kx])
        return j

    for k in range(1, n):
        go(remote(gs.at[s], gs.at[s], gs_sem.at[k], gr_sem.at[k], (s + k) % n, r))

    @pl.when(s == n - 1)
    def _():
        window[pl.ds(rows, HALO), :] = jnp.zeros((HALO, width), BF16)

    square0 = lax.broadcasted_iota(jnp.int32, (patches, patches), 0)
    square1 = lax.broadcasted_iota(jnp.int32, (patches, patches), 1)
    local[1].wait()
    first = (st[...].reshape(1, patches) - s * rows).astype(F32)
    low = jnp.sum(jnp.where(square0 == square1, first, 0.0), axis=1, keepdims=True)
    high = jnp.sum(jnp.where(square0 + 1 == square1, first, 0.0), axis=1, keepdims=True)
    line = lax.broadcasted_iota(jnp.int32, (patches, 1), 0)
    high = jnp.where(line == patches - 1, (rows + straddle[0]).astype(F32), high)
    place = lax.broadcasted_iota(jnp.int32, (patches, rows + HALO), 1).astype(F32)
    member = (place >= low) & (place < high)
    count = high - low

    local[0].wait()
    local[3].wait()

    @pl.when(s < n - 1)
    def _():
        halo.wait_recv()

    for t in range(1, min(nz, 3)):
        pass_first((t, 0))
        if t == 1:
            send_rest(0, flip(zi, 1) * nx + xi)
    for k in range(1, nx):
        send_rest(k, seq_of(0, k))

    whole = window[...]
    keys = dot(whole, kw[...]).astype(BF16)
    query = (dot(member.astype(BF16), whole) / count).astype(BF16)
    scale = F32(1.0 / math.sqrt(LHD))
    for h in range(width // LHD):
        part = slice(h * LHD, (h + 1) * LHD)
        pg[s, :, part] = softmax_dot(
            dot_t(query[:, part], keys[:, part]) * scale, member, whole[:, part]
        )
    for kz in range(1, nz):
        go(remote(pg.at[s], pg.at[s], ps_sem.at[kz, 0], pr_sem.at[kz, 0], seq_of(kz, 0), r))
    for kx in range(1, nx):
        go(remote(pg.at[s], pg.at[s], ps_sem.at[0, kx], pr_sem.at[0, kx], seq_of(0, kx), r))

    for k in range(1, nx):
        pass_first((0, k))
    for t in range(3, nz):
        pass_first((t, 0))
    late = [(t, kx) for t in range(1, nz) for kx in range(1, nx)]
    for o in late[:1]:
        pass_first(o)
    for kz in range(1, nz):
        j = seq_of(kz, 0)
        wait_for(pg.at[j], pr_sem.at[kz, 0])
        for kx in range(1, nx):
            go(remote(pg.at[j], pg.at[j], ps_sem.at[kz, kx], pr_sem.at[kz, kx], seq_of(0, kx), r))
    for o in late[1:2]:
        pass_first(o)

    for kz in range(nz):
        for kx in range(1, nx):
            wait_for(pg.at[s], pr_sem.at[kz, kx])
    for k in range(1, n):
        wait_for(gs.at[s], gr_sem.at[k])
    pooled = pg[...].reshape(n * patches, width)

    def project(j, squares, fresh):
        weight = ow[j].reshape(width, cols)
        embed = dot(pooled, weight)
        squares = squares + jnp.sum(embed * embed, axis=1, keepdims=True)
        scaled = (embed * gs[j]).astype(BF16)
        for t in range(3):
            span = slice(t * cols, (t + 1) * cols)
            term = dot(scaled, w[t, j])
            if fresh:
                acc[:, span] = term
            else:
                acc[:, span] = acc[:, span] + term
        return squares

    rest = [(1, 0)] if nz > 1 else []
    rest += [(0, kx) for kx in range(1, nx)] + [(t, 0) for t in range(2, nz)] + late
    still, ready, steps = late[2:], [], []
    for i, o in enumerate(rest):
        steps.append((pass_rest, o))
        if i < len(still):
            steps.append((pass_first, still[i]))
        if i >= 2:
            steps.append((None, ready.pop(0)))
        ready.append(o)
    steps += [(None, o) for o in ready]

    local[4].wait()
    w_copy.wait()
    squares = project(s, jnp.zeros((n * patches, 1), F32), True)
    for act, o in steps:
        if act is None:
            squares = project(arrived(o), squares, False)
        else:
            act(o)

    total = n * patches
    rstd = lax.rsqrt(squares / F32(model) + epsilon)
    causal = lax.broadcasted_iota(jnp.int32, (total, total), 0) >= lax.broadcasted_iota(
        jnp.int32, (total, total), 1
    )
    scale = F32(1.0 / math.sqrt(HD))
    own = []
    for h in range(heads):
        q, k, v = (
            (acc[:, t * cols + h * HD : t * cols + (h + 1) * HD] * rstd).astype(BF16)
            for t in range(3)
        )
        att[h] = softmax_dot(dot_t(q, k) * scale, causal, v).reshape(n, patches, HD)
        span = pl.ds(pl.multiple_of(s * cols + h * HD, HD), HD)
        for k in range(1, n):
            j = (s + k) % n
            go(remote(att.at[h, j], out.at[:, span], as_sem.at[h, k], ar_sem.at[h, k], j, r))
        own.append(pltpu.make_async_copy(att.at[h, s], out.at[:, span], as_sem.at[h, 0]))
        own[-1].start()

    for copy in own:
        copy.wait()
    for h in range(heads):
        for k in range(1, n):
            span = pl.ds(pl.multiple_of(((s + n - k) % n) * cols + h * HD, HD), HD)
            wait_for(out.at[:, span], ar_sem.at[h, k])
    for copy in sent:
        copy.wait_send()
    for cond, copy in maybe:
        pl.when(cond)(copy.wait_send)

    @pl.when(s > 0)
    def _():
        halo.wait_send()


def split_seq(n):
    power = 1
    while power * power < n:
        power *= 2
    return (power, n // power) if n % power == 0 else (n, 1)


def shards(states, starts, straddle, key_weight, out_weight, norm_gain, attn_weight):
    n, reps = lax.axis_size("seq"), lax.axis_size("rep")
    nz, nx = split_seq(n)
    ny = reps // CORES
    rows, width = states.shape
    patches = starts.shape[0]
    model, three, cols = attn_weight.shape
    heads = cols // HD
    total = n * patches
    w = attn_weight.transpose(1, 0, 2).reshape(three, n, model // n, cols)
    any_space = pl.BlockSpec(memory_space=pl.ANY)
    smem = pl.BlockSpec(memory_space=pltpu.SMEM)
    dma = pltpu.SemaphoreType.DMA
    flops = 2 * total * (model * three * cols + width * model)
    return pl.pallas_call(
        functools.partial(kernel, nz, nx, ny),
        out_shape=jax.ShapeDtypeStruct((patches, model), BF16),
        in_specs=[any_space, any_space, smem, any_space, any_space, any_space, any_space],
        out_specs=pl.BlockSpec(memory_space=pltpu.VMEM),
        scratch_shapes=[
            pltpu.VMEM((rows + HALO, width), BF16),
            pltpu.VMEM(key_weight.shape, BF16),
            pltpu.VMEM((n, CORES, ny, width // reps, cols), BF16),
            pltpu.VMEM(w.shape, BF16),
            pltpu.VMEM((n, patches, width), BF16),
            pltpu.VMEM((cols,), BF16),
            pltpu.VMEM((n, 1, cols), F32),
            pltpu.VMEM((patches,), jnp.int32),
            pltpu.VMEM((total, three * cols), F32),
            pltpu.VMEM((heads, n, patches, HD), BF16),
            dma((5,)), dma, dma((2,)),
            dma((nz, 2)), dma((nz,)), dma((nz, nx)), dma((nz, nx)), dma((nx, ny)), dma((nx, ny)),
            dma((ny, nz, nx)), dma((ny, nz, nx)), dma((ny, nz, nx)), dma((ny, nz, nx)),
            dma((nz, nx)), dma((nz, nx)), dma((n,)), dma((n,)), dma((heads, n)), dma((heads, n)),
        ],
        compiler_params=pltpu.CompilerParams(
            collective_id=0, has_side_effects=True, vmem_limit_bytes=60 * 1024 * 1024
        ),
        cost_estimate=pl.CostEstimate(
            flops=flops, bytes_accessed=w.size * 2, transcendentals=0
        ),
    )(
        states, starts, straddle, key_weight,
        out_weight.reshape(CORES, ny, width // reps, cols), norm_gain, w,
    )


def solution(mesh):
    placed = (
        P(("rep", "seq"), None),
        P(("rep", "seq")),
        P(("rep", "seq")),
        P(),
        P(None, "seq"),
        P("seq"),
        P(None, None, "seq"),
    )
    return jax.shard_map(
        shards, mesh=mesh, in_specs=placed, out_specs=P(("rep", "seq"), None), check_vma=False
    )
```

```python
import functools
import math

import jax
import jax.numpy as jnp
from jax import lax
from jax.experimental import pallas as pl
from jax.experimental.pallas import tpu as pltpu
from jax.sharding import PartitionSpec as P

HD = 128
LHD = 128
HALO = 64
CORES = 2
CHUNKS = 2

epsilon = 1e-05

BF16 = jnp.bfloat16
F32 = jnp.float32


def dot(a, b):
    return jnp.dot(a, b, preferred_element_type=F32)


def dot_t(a, b):
    return lax.dot_general(a, b, (((1,), (1,)), ((), ())), preferred_element_type=F32)


def softmax_dot(scores, keep, values):
    scores = jnp.where(keep, scores, F32(-1e30))
    peak = jnp.max(scores, axis=-1, keepdims=True)
    expo = jnp.where(keep, jnp.exp(scores - peak), F32(0.0))
    total = jnp.sum(expo, axis=-1, keepdims=True)
    return dot((expo / total).astype(BF16), values).astype(BF16)


def kernel(
    nz, nx, ny,
    states, starts, straddle, key_weight, out_weight, gain, attn_weight,
    out,
    window, kw, ow, w, pg, gv, gs, st, acc, att,
    l_sem, w_sem, h_sem,
    zs_sem, zr_sem, xs_sem, xr_sem, es_sem, er_sem, ys_sem, yr_sem, cs_sem, cr_sem,
    ps_sem, pr_sem, gs_sem, gr_sem, as_sem, ar_sem,
):
    n = nz * nx
    s = lax.axis_index("seq")
    r = lax.axis_index("rep")
    zi, xi = s // nx, s % nx
    yi, ci = r // CORES, r % CORES
    other = yi * CORES + (1 - ci)
    rows, width = states.shape
    patches = starts.shape[0]
    cols = out_weight.shape[4]
    heads = cols // HD
    model = cols * n

    def flip(index, mask):
        bit = 1
        for _ in range(mask.bit_length()):
            if mask & bit:
                index = index + (1 - 2 * ((index // bit) % 2)) * bit
            bit *= 2
        return index

    def seq_of(kz, kx):
        return flip(zi, kz) * nx + (xi + nx + kx) % nx

    def y_of(ky):
        return (yi + ny + ky) % ny

    def rep_of(ky):
        return y_of(ky) * CORES + ci

    def remote(src, dst, send, recv, seq, rep):
        return pltpu.make_async_remote_copy(
            src_ref=src, dst_ref=dst, send_sem=send, recv_sem=recv,
            device_id={"seq": seq, "rep": rep}, device_id_type=pl.DeviceIdType.MESH,
        )

    barrier = pltpu.get_barrier_semaphore()

    def greet(seq, rep):
        pl.semaphore_signal(
            barrier, inc=1, device_id={"seq": seq, "rep": rep},
            device_id_type=pl.DeviceIdType.MESH,
        )

    for k in range(1, n):
        greet((s + k) % n, r)
    for k in range(1, ny):
        greet(s, rep_of(k))
    greet(s, other)

    local = [
        pltpu.make_async_copy(states, window.at[pl.ds(0, rows)], l_sem.at[0]),
        pltpu.make_async_copy(starts, st, l_sem.at[1]),
        pltpu.make_async_copy(gain, gv, l_sem.at[2]),
        pltpu.make_async_copy(key_weight, kw, l_sem.at[3]),
        pltpu.make_async_copy(out_weight, ow.at[s], l_sem.at[4]),
    ]
    for copy in local:
        copy.start()
    w_copy = pltpu.make_async_copy(attn_weight, w, w_sem)
    w_copy.start()
    local[2].wait()
    gs[s] = gv[...].astype(F32).reshape(1, cols)

    pl.semaphore_wait(barrier, n - 1 + ny - 1 + 1)

    left = (s + n - 1) % n
    halo = remote(
        states.at[pl.ds(0, HALO)], window.at[pl.ds(rows, HALO)],
        h_sem.at[0], h_sem.at[1], left, r,
    )

    @pl.when(s > 0)
    def _():
        halo.start()

    sent, maybe = [], []

    def go(copy):
        copy.start()
        sent.append(copy)

    def go_if(cond, copy):
        @pl.when(cond)
        def _():
            copy.start()

        maybe.append((cond, copy))

    even = 1 - zi % 2
    short = jnp.minimum(zi, nz - 1 - zi)

    def near(t):
        if t == 0:
            return zi
        ahead = even if t % 2 == 1 else 1 - even
        both = zi + (2 * ahead - 1) * ((t + 1) // 2)
        lone = jnp.where(zi * 2 < nz, zi + t - short, zi - t + short)
        return jnp.where(t <= 2 * short, both, lone)

    line_z = [near(t) for t in range(nz)]

    def shard_of(o):
        return line_z[o[0]] * nx + (xi + nx - o[1]) % nx

    def wait_for(ref, sem):
        pltpu.make_async_copy(ref, ref, sem).wait()

    whole_ones = [(0, kx) for kx in range(1, nx)] + ([(1, 0)] if nz > 1 else [])

    for c in range(CHUNKS):
        mine = out_weight.at[ci, yi, c]
        here = ow.at[s, ci, yi, c]
        for side in range(2):
            z_to = zi + 2 * side - 1
            go_if(
                (z_to >= 0) & (z_to < nz),
                remote(mine, here, zs_sem.at[0, side, c], zr_sem.at[zi, c], z_to * nx + xi, r),
            )
        for k in range(1, nx):
            go(remote(mine, here, xs_sem.at[0, k, c], xr_sem.at[0, k, c], seq_of(0, k), r))

    def send_rest(k, seq):
        for ky in range(1, ny):
            part = y_of(-ky)
            for c in range(CHUNKS):
                go(remote(
                    out_weight.at[ci, part, c], ow.at[s, ci, part, c],
                    es_sem.at[k, ky, c], er_sem.at[k, ky, c], seq, r,
                ))

    def pass_first(o):
        for c in range(CHUNKS):
            pass_chunk(o, c)

    def pass_chunk(o, c):
        t, kx = o
        j = shard_of(o)
        piece = ow.at[j, ci, yi, c]
        wait_for(piece, zr_sem.at[line_z[t], c] if kx == 0 else xr_sem.at[t, kx, c])
        if kx == 0:
            z_to = jnp.where(line_z[t] < zi, zi + 1, zi - 1)
            go_if(
                (z_to >= 0) & (z_to < nz),
                remote(piece, piece, zs_sem.at[t, 0, c], zr_sem.at[line_z[t], c], z_to * nx + xi, r),
            )
            for k in range(1, nx):
                go(remote(piece, piece, xs_sem.at[t, k, c], xr_sem.at[t, k, c], seq_of(0, k), r))
        if o not in whole_ones:
            for ky in range(1, ny):
                go(remote(piece, piece, ys_sem.at[ky, t, kx, c], yr_sem.at[ky, t, kx, c], s, rep_of(ky)))
        go(remote(piece, piece, cs_sem.at[0, t, kx, c], cr_sem.at[0, t, kx, c], s, other))

    def pass_rest(o):
        t, kx = o
        for ky in range(1, ny):
            for c in range(CHUNKS):
                piece = ow.at[shard_of(o), ci, y_of(-ky), c]
                wait_for(piece, er_sem.at[kx, ky, c] if o in whole_ones else yr_sem.at[ky, t, kx, c])
                go(remote(piece, piece, cs_sem.at[ky, t, kx, c], cr_sem.at[ky, t, kx, c], s, other))

    def arrived(o):
        t, kx = o
        j = shard_of(o)
        for ky in range(ny):
            for c in range(CHUNKS):
                wait_for(ow.at[j, 1 - ci, y_of(-ky), c], cr_sem.at[ky, t, kx, c])
        return j

    for k in range(1, n):
        go(remote(gs.at[s], gs.at[s], gs_sem.at[k], gr_sem.at[k], (s + k) % n, r))

    @pl.when(s == n - 1)
    def _():
        window[pl.ds(rows, HALO), :] = jnp.zeros((HALO, width), BF16)

    square0 = lax.broadcasted_iota(jnp.int32, (patches, patches), 0)
    square1 = lax.broadcasted_iota(jnp.int32, (patches, patches), 1)
    local[1].wait()
    first = (st[...].reshape(1, patches) - s * rows).astype(F32)
    low = jnp.sum(jnp.where(square0 == square1, first, 0.0), axis=1, keepdims=True)
    high = jnp.sum(jnp.where(square0 + 1 == square1, first, 0.0), axis=1, keepdims=True)
    line = lax.broadcasted_iota(jnp.int32, (patches, 1), 0)
    high = jnp.where(line == patches - 1, (rows + straddle[0]).astype(F32), high)
    place = lax.broadcasted_iota(jnp.int32, (patches, rows + HALO), 1).astype(F32)
    member = (place >= low) & (place < high)
    count = high - low

    local[0].wait()
    local[3].wait()

    @pl.when(s < n - 1)
    def _():
        halo.wait_recv()

    for t in range(1, min(nz, 3)):
        pass_first((t, 0))
        if t == 1:
            send_rest(0, flip(zi, 1) * nx + xi)
    for k in range(1, nx):
        send_rest(k, seq_of(0, k))

    whole = window[...]
    keys = dot(whole, kw[...]).astype(BF16)
    query = (dot(member.astype(BF16), whole) / count).astype(BF16)
    scale = F32(1.0 / math.sqrt(LHD))
    for h in range(width // LHD):
        part = slice(h * LHD, (h + 1) * LHD)
        pg[s, :, part] = softmax_dot(
            dot_t(query[:, part], keys[:, part]) * scale, member, whole[:, part]
        )
    for kz in range(1, nz):
        go(remote(pg.at[s], pg.at[s], ps_sem.at[kz, 0], pr_sem.at[kz, 0], seq_of(kz, 0), r))
    for kx in range(1, nx):
        go(remote(pg.at[s], pg.at[s], ps_sem.at[0, kx], pr_sem.at[0, kx], seq_of(0, kx), r))

    for k in range(1, nx):
        pass_first((0, k))
    for t in range(3, nz):
        pass_first((t, 0))
    late = [(t, kx) for t in range(1, nz) for kx in range(1, nx)]
    for o in late[:1]:
        pass_first(o)
    for kz in range(1, nz):
        j = seq_of(kz, 0)
        wait_for(pg.at[j], pr_sem.at[kz, 0])
        for kx in range(1, nx):
            go(remote(pg.at[j], pg.at[j], ps_sem.at[kz, kx], pr_sem.at[kz, kx], seq_of(0, kx), r))
    for o in late[1:2]:
        pass_first(o)

    for kz in range(nz):
        for kx in range(1, nx):
            wait_for(pg.at[s], pr_sem.at[kz, kx])
    for k in range(1, n):
        wait_for(gs.at[s], gr_sem.at[k])
    pooled = pg[...].reshape(n * patches, width)

    def project(j, squares, fresh):
        weight = ow[j].reshape(width, cols)
        embed = dot(pooled, weight)
        squares = squares + jnp.sum(embed * embed, axis=1, keepdims=True)
        scaled = (embed * gs[j]).astype(BF16)
        for t in range(3):
            span = slice(t * cols, (t + 1) * cols)
            term = dot(scaled, w[t, j])
            if fresh:
                acc[:, span] = term
            else:
                acc[:, span] = acc[:, span] + term
        return squares

    rest = [(1, 0)] if nz > 1 else []
    rest += [(0, kx) for kx in range(1, nx)] + [(t, 0) for t in range(2, nz)] + late
    still, ready, steps = late[2:], [], []
    for i, o in enumerate(rest):
        steps.append((pass_rest, o))
        if i < len(still):
            steps.append((pass_first, still[i]))
        if i >= 2:
            steps.append((None, ready.pop(0)))
        ready.append(o)
    steps += [(None, o) for o in ready]

    local[4].wait()
    w_copy.wait()
    squares = project(s, jnp.zeros((n * patches, 1), F32), True)
    for act, o in steps:
        if act is None:
            squares = project(arrived(o), squares, False)
        else:
            act(o)

    total = n * patches
    rstd = lax.rsqrt(squares / F32(model) + epsilon)
    causal = lax.broadcasted_iota(jnp.int32, (total, total), 0) >= lax.broadcasted_iota(
        jnp.int32, (total, total), 1
    )
    scale = F32(1.0 / math.sqrt(HD))
    own = []
    for h in range(heads):
        q, k, v = (
            (acc[:, t * cols + h * HD : t * cols + (h + 1) * HD] * rstd).astype(BF16)
            for t in range(3)
        )
        att[h] = softmax_dot(dot_t(q, k) * scale, causal, v).reshape(n, patches, HD)
        span = pl.ds(pl.multiple_of(s * cols + h * HD, HD), HD)
        for k in range(1, n):
            j = (s + k) % n
            go(remote(att.at[h, j], out.at[:, span], as_sem.at[h, k], ar_sem.at[h, k], j, r))
        own.append(pltpu.make_async_copy(att.at[h, s], out.at[:, span], as_sem.at[h, 0]))
        own[-1].start()

    for copy in own:
        copy.wait()
    for h in range(heads):
        for k in range(1, n):
            span = pl.ds(pl.multiple_of(((s + n - k) % n) * cols + h * HD, HD), HD)
            wait_for(out.at[:, span], ar_sem.at[h, k])
    for copy in sent:
        copy.wait_send()
    for cond, copy in maybe:
        pl.when(cond)(copy.wait_send)

    @pl.when(s > 0)
    def _():
        halo.wait_send()


def split_seq(n):
    power = 1
    while power * power < n:
        power *= 2
    return (power, n // power) if n % power == 0 else (n, 1)


def shards(states, starts, straddle, key_weight, out_weight, norm_gain, attn_weight):
    n, reps = lax.axis_size("seq"), lax.axis_size("rep")
    nz, nx = split_seq(n)
    ny = reps // CORES
    rows, width = states.shape
    patches = starts.shape[0]
    model, three, cols = attn_weight.shape
    heads = cols // HD
    total = n * patches
    w = attn_weight.transpose(1, 0, 2).reshape(three, n, model // n, cols)
    any_space = pl.BlockSpec(memory_space=pl.ANY)
    smem = pl.BlockSpec(memory_space=pltpu.SMEM)
    dma = pltpu.SemaphoreType.DMA
    flops = 2 * total * (model * three * cols + width * model)
    return pl.pallas_call(
        functools.partial(kernel, nz, nx, ny),
        out_shape=jax.ShapeDtypeStruct((patches, model), BF16),
        in_specs=[any_space, any_space, smem, any_space, any_space, any_space, any_space],
        out_specs=pl.BlockSpec(memory_space=pltpu.VMEM),
        scratch_shapes=[
            pltpu.VMEM((rows + HALO, width), BF16),
            pltpu.VMEM(key_weight.shape, BF16),
            pltpu.VMEM((n, CORES, ny, CHUNKS, width // reps // CHUNKS, cols), BF16),
            pltpu.VMEM(w.shape, BF16),
            pltpu.VMEM((n, patches, width), BF16),
            pltpu.VMEM((cols,), BF16),
            pltpu.VMEM((n, 1, cols), F32),
            pltpu.VMEM((patches,), jnp.int32),
            pltpu.VMEM((total, three * cols), F32),
            pltpu.VMEM((heads, n, patches, HD), BF16),
            dma((5,)), dma, dma((2,)),
            dma((nz, 2, CHUNKS)), dma((nz, CHUNKS)), dma((nz, nx, CHUNKS)), dma((nz, nx, CHUNKS)),
            dma((nx, ny, CHUNKS)), dma((nx, ny, CHUNKS)),
            *(dma((ny, nz, nx, CHUNKS)) for _ in range(4)),
            dma((nz, nx)), dma((nz, nx)), dma((n,)), dma((n,)), dma((heads, n)), dma((heads, n)),
        ],
        compiler_params=pltpu.CompilerParams(
            collective_id=0, has_side_effects=True, vmem_limit_bytes=60 * 1024 * 1024
        ),
        cost_estimate=pl.CostEstimate(
            flops=flops, bytes_accessed=w.size * 2, transcendentals=0
        ),
    )(
        states, starts, straddle, key_weight,
        out_weight.reshape(CORES, ny, CHUNKS, width // reps // CHUNKS, cols), norm_gain, w,
    )


def solution(mesh):
    placed = (
        P(("rep", "seq"), None),
        P(("rep", "seq")),
        P(("rep", "seq")),
        P(),
        P(None, "seq"),
        P("seq"),
        P(None, None, "seq"),
    )
    return jax.shard_map(
        shards, mesh=mesh, in_specs=placed, out_specs=P(("rep", "seq"), None), check_vma=False
    )
```
